32 devices in a mesh: dp: 8 (over z, y), seq: 4 (over x, core).
Axes of the slice: x: 2, y: 2, z: 4, core: 2. Of those that a mesh axis runs over, the one named last changes fastest.
Arguments:
- slot_tokens: bfloat16 [104, 256, 1152], P('dp', 'seq'), may hold values from -12 to 12
- modulation: float32 [8, 6, 1152], P('dp'), may hold values from -2.5 to 2.5
- counts: int32 [8], replicated, may hold values from 1 to 13, as said below
- dest: int32 [8, 13], replicated, may hold values from 0 to 55, as said below
- qkv_spatial: bfloat16 [1152, 1728], replicated, may hold values from -4 to 4
- out_spatial: bfloat16 [576, 1152], replicated, may hold values from -0.25 to 0.25
- qkv_temporal: bfloat16 [1152, 1728], replicated, may hold values from -4 to 4
- out_temporal: bfloat16 [576, 1152], replicated, may hold values from -0.25 to 0.25
Outputs:
- video_out: bfloat16 [56, 256, 1152], P('dp', 'seq')
The draws below stay inside these ranges and needn't reach their ends.
Inputs may be any that keep to these rules, and one draw needn't show every extreme that they name: Group g holds blocks in slots 0 to counts[g] - 1; the counts sum to 56; some group holds 13 blocks. Over the slots q below counts[g] of all groups g, dest[g, q] takes every value 0 to 55 exactly once; one group sends at most 2 blocks to one video, and some group sends 2; entries at slots from counts[g] on are arbitrary values of the same range.
All inputs are finite; a program needn't handle non-finite values.
Results may differ from the reference program's by a relative error of at most 0.0057.
Values may be sent and summed in bfloat16 or wider, within the bound.
A program may use at most 64 MiB of HBM per device.

```python
import math
import jax
import jax.numpy as jnp
from jax import lax

D = 1152
HEADS = 8
HEAD_DIM = 72
PATCHES = 64
NFD = 7
HD = 576
SLOTS = 13
PMAX = 16
N_DP = 8
N_SEQ = 4


def route_plan(base_key):
    group_count = N_DP
    plan_key = jax.random.fold_in(base_key, 404)
    pair_order = jax.random.permutation(jax.random.fold_in(plan_key, 1), group_count)
    changes = jax.random.randint(jax.random.fold_in(plan_key, 2), (group_count // 2,), 0, NFD)
    changes = changes.at[0].set(SLOTS - NFD).astype(jnp.int32)
    counts = jnp.full((group_count,), NFD, jnp.int32)
    counts = counts.at[pair_order[0::2]].add(changes).at[pair_order[1::2]].add(-changes)
    order = jax.random.permutation(jax.random.fold_in(plan_key, 3), group_count)
    ordered = counts[order]
    offsets_ordered = jnp.cumsum(ordered).astype(jnp.int32) - ordered
    offsets = jnp.zeros((group_count,), jnp.int32).at[order].set(offsets_ordered)
    video_order = jax.random.permutation(jax.random.fold_in(plan_key, 4), group_count).astype(jnp.int32)
    rotations = jax.random.randint(jax.random.fold_in(plan_key, 5), (group_count,), 0, NFD)
    slot_ids = jnp.arange(SLOTS, dtype=jnp.int32)
    items = offsets[:, None] + slot_ids[None, :]
    videos = video_order[items % group_count]
    positions = (items // group_count + rotations[videos]) % NFD
    live_dest = videos * NFD + positions
    filler = jax.random.randint(jax.random.fold_in(plan_key, 6), (group_count, SLOTS), 0, group_count * NFD)
    dest = jnp.where(slot_ids[None, :] < counts[:, None], live_dest, filler)
    return (counts.astype(jnp.int32), dest.astype(jnp.int32))


def draw_counts(key, part):
    return route_plan(key)[0]


def draw_dest(key, part):
    return route_plan(key)[1]


def draw_slot_tokens(key, part):
    token_key = jax.random.fold_in(key, 303)
    rows = N_DP * SLOTS
    columns = N_SEQ * PATCHES
    base = jax.random.normal(jax.random.fold_in(token_key, 1), (rows, columns, D), jnp.float32)
    row_scale = jnp.exp(jax.random.uniform(jax.random.fold_in(token_key, 3), (rows, columns, 1), jnp.float32, math.log(0.3), math.log(3.0)))
    column_scale = jnp.exp(jax.random.uniform(jax.random.fold_in(token_key, 4), (D,), jnp.float32, math.log(0.5), math.log(2.0)))
    return jnp.clip(base * row_scale * column_scale, -12.0, 12.0).astype(jnp.bfloat16)


def projection_draw(weight_key):
    entries = jax.random.normal(jax.random.fold_in(weight_key, 1), (D, 3, HEADS, HEAD_DIM), jnp.float32) / math.sqrt(D)
    return jnp.clip(entries.reshape(D, 3 * HEADS * HEAD_DIM), -4.0, 4.0).astype(jnp.bfloat16)


def draw_qkv_spatial(key, part):
    return projection_draw(jax.random.fold_in(key, 101))


def draw_qkv_temporal(key, part):
    return projection_draw(jax.random.fold_in(key, 202))


def block_levels(key, shape, cuts, smallest, largest):
    gain, own = 1.0, jax.random.fold_in(key, 6)
    for dim, shards_of in cuts:
        steps = jnp.exp(jax.random.uniform(jax.random.fold_in(own, dim), (shards_of,), jnp.float32, smallest / len(cuts), largest / len(cuts)))
        gain = gain * jnp.repeat(steps, shape[dim] // shards_of).reshape([-1 if axis == dim else 1 for axis in range(len(shape))])
    return gain


def gaussian(stream_key, shape, width, reach, shards=(), kind=jnp.bfloat16):
    drawn = width * jax.random.normal(stream_key, shape, jnp.float32)
    if shards:
        drawn = drawn * block_levels(stream_key, shape, shards, -0.22, 0.18)
    return jnp.clip(drawn, -reach, reach).astype(kind)


def setup_inputs(seed: int = 0) -> dict:
    splits = jax.random.split(jax.random.key(seed), 9)
    slot_tokens = draw_slot_tokens(jax.random.fold_in(splits[8], 71), 0)
    modulation = gaussian(splits[1], (N_DP, 6, D), 0.5, 2.5, ((0, 8),), jnp.float32)
    counts = draw_counts(jax.random.fold_in(splits[8], 71), 0)
    dest = draw_dest(jax.random.fold_in(splits[8], 71), 0)
    qkv_spatial = draw_qkv_spatial(jax.random.fold_in(splits[8], 71), 0)
    out_spatial = gaussian(splits[5], (HD, D), HD ** -0.5, 0.25)
    qkv_temporal = draw_qkv_temporal(jax.random.fold_in(splits[8], 71), 0)
    out_temporal = gaussian(splits[7], (HD, D), HD ** -0.5, 0.25)
    return dict(slot_tokens=slot_tokens, modulation=modulation, counts=counts, dest=dest, qkv_spatial=qkv_spatial, out_spatial=out_spatial, qkv_temporal=qkv_temporal, out_temporal=out_temporal)


epsilon = 1e-06

def norm_mod(tokens, shift_row, scale_row):
    values = tokens.astype(jnp.float32)
    center = values - lax.optimization_barrier(jnp.mean(values, axis=-1, keepdims=True))
    spread = lax.optimization_barrier(jnp.mean(center * center, axis=-1, keepdims=True))
    return (center * lax.rsqrt(spread + epsilon) * (1.0 + scale_row) + shift_row).astype(jnp.bfloat16)

def attend(qkv_rows, batch_count, length):
    parts = qkv_rows.astype(jnp.float32).reshape(batch_count, length, 3, HEADS, HEAD_DIM)
    factor = 1.0 / math.sqrt(HEAD_DIM)
    scores = jnp.einsum('bqhs,bkhs->bhqk', parts[:, :, 0], parts[:, :, 1]) * factor
    highest = lax.optimization_barrier(jnp.max(scores, axis=-1, keepdims=True))
    raised = jnp.exp(scores - highest)
    weights = (raised / lax.optimization_barrier(jnp.sum(raised, axis=-1, keepdims=True))).astype(jnp.bfloat16)
    mixed = jnp.einsum('bhqk,bkhs->bqhs', weights.astype(jnp.float32), parts[:, :, 2])
    return mixed.astype(jnp.bfloat16).reshape(batch_count * length, HEADS * HEAD_DIM)

def reference(slot_tokens, modulation, counts, dest, qkv_spatial, out_spatial, qkv_temporal, out_temporal):
    slot_ids = jnp.arange(SLOTS, dtype=jnp.int32)
    live_slots = slot_ids[None, :] < counts[:, None]
    targets = jnp.where(live_slots, dest, N_DP * NFD).astype(jnp.int32).reshape(-1)
    anchors = (jnp.arange(N_DP, dtype=jnp.int32)[:, None] * SLOTS + slot_ids[None, :]).astype(jnp.int32).reshape(-1)
    source_of = jnp.zeros((N_DP * NFD,), jnp.int32).at[targets].set(anchors, mode='drop')
    video_blocks = jnp.take(slot_tokens, source_of, axis=0)
    videos = video_blocks.reshape(N_DP, NFD * N_SEQ, PATCHES, D)

    def one_video(pair):
        video_frames, video_modulation = pair
        frame_count = video_frames.shape[0]
        normed = norm_mod(video_frames, video_modulation[0], video_modulation[1])
        qkv_rows = jnp.dot(normed.reshape(-1, D), qkv_spatial, preferred_element_type=jnp.float32).astype(jnp.bfloat16)
        mixed = attend(qkv_rows, frame_count, PATCHES)
        projected = jnp.dot(mixed, out_spatial, preferred_element_type=jnp.float32).reshape(frame_count, PATCHES, D)
        after_spatial = (video_frames.astype(jnp.float32) + video_modulation[2] * projected).astype(jnp.bfloat16)
        grouped = after_spatial.reshape(frame_count, N_SEQ, PMAX, D)
        grouped = grouped.transpose(1, 0, 2, 3).reshape(N_SEQ, frame_count * PMAX, D)
        normed_two = norm_mod(grouped, video_modulation[3], video_modulation[4])
        qkv_two = jnp.dot(normed_two.reshape(-1, D), qkv_temporal, preferred_element_type=jnp.float32).astype(jnp.bfloat16)
        qkv_two = qkv_two.reshape(N_SEQ, frame_count, PMAX, 3 * HD).transpose(0, 2, 1, 3).reshape(N_SEQ * PMAX * frame_count, 3 * HD)
        mixed_two = attend(qkv_two, N_SEQ * PMAX, frame_count)
        mixed_two = mixed_two.reshape(N_SEQ, PMAX, frame_count, HD).transpose(0, 2, 1, 3).reshape(N_SEQ * frame_count * PMAX, HD)
        projected_two = jnp.dot(mixed_two, out_temporal, preferred_element_type=jnp.float32).reshape(N_SEQ, frame_count * PMAX, D)
        result = (grouped.astype(jnp.float32) + video_modulation[5] * projected_two).astype(jnp.bfloat16)
        return result.reshape(N_SEQ, frame_count, PMAX, D).transpose(1, 0, 2, 3).reshape(frame_count, PATCHES, D)
    outputs = lax.map(one_video, (videos, modulation))
    return outputs.reshape(N_DP * NFD, N_SEQ * PATCHES, D)
```

```python
import functools
import math

import jax
import jax.numpy as jnp
from jax import lax
from jax.experimental import pallas as pl
from jax.experimental.pallas import tpu as pltpu
from jax.sharding import PartitionSpec as P

HEADS = 8
HEAD_DIM = 72
NFD = 7
EPSILON = 1e-06
BATCH = 4
HALF = 8
MESH = pl.DeviceIdType.MESH


def norm_mod(values, shift_row, scale_row):
    center = values - jnp.mean(values, axis=-1, keepdims=True)
    spread = jnp.mean(center * center, axis=-1, keepdims=True)
    return (center * lax.rsqrt(spread + EPSILON) * (1.0 + scale_row) + shift_row).astype(jnp.bfloat16)


def attend(qkv, same):
    width = HEADS * HEAD_DIM
    factor = 1.0 / math.sqrt(HEAD_DIM)
    mixed = []
    for head in range(HEADS):
        at = head * HEAD_DIM
        q = qkv[:, at : at + HEAD_DIM]
        k = qkv[:, width + at : width + at + HEAD_DIM]
        v = qkv[:, 2 * width + at : 2 * width + at + HEAD_DIM]
        scores = lax.dot_general(q, k, (((1,), (1,)), ((), ())), preferred_element_type=jnp.float32)
        scores = jnp.where(same, scores * factor, -1e30)
        raised = jnp.exp(scores - jnp.max(scores, axis=-1, keepdims=True))
        weights = (raised * (1.0 / jnp.sum(raised, axis=-1, keepdims=True))).astype(jnp.bfloat16)
        mixed.append(jnp.dot(weights, v, preferred_element_type=jnp.float32))
    return jnp.concatenate(mixed, axis=-1)


def kernel(
    groups, shards, rooms,
    counts_ref, dest_ref, tok_ref, mod_ref, wqs_hbm, wos_hbm, wqt_hbm, wot_hbm,
    out_ref,
    wqs, wos, wqt, wot, send, arr, arr2, rows, res,
    w_sem, dp_send, dp_recv, sq_send, sq_recv, home_send, home_recv,
):
    group = lax.axis_index("dp")
    shard = lax.axis_index("seq")
    slots = tok_ref.shape[0]
    widest, width = tok_ref.shape[2], tok_ref.shape[3]
    patches = shards * widest
    room_slots = rooms * groups
    batches = room_slots // BATCH
    frames = NFD * shards

    barrier = pltpu.get_barrier_semaphore()

    def greet_dp(j, c):
        pl.semaphore_signal(
            barrier, inc=1, device_id=(lax.rem(group + 1 + j, groups), shard), device_id_type=MESH
        )
        return c

    def greet_seq(i, c):
        pl.semaphore_signal(
            barrier, inc=1, device_id=(group, lax.rem(shard + 1 + i, shards)), device_id_type=MESH
        )
        return c

    lax.fori_loop(0, groups - 1, greet_dp, 0)
    lax.fori_loop(0, shards - 1, greet_seq, 0)

    loads = [
        pltpu.make_async_copy(src, dst, w_sem.at[i])
        for i, (src, dst) in enumerate(
            ((wqs_hbm, wqs), (wos_hbm, wos), (wqt_hbm, wqt), (wot_hbm, wot))
        )
    ]
    for load in loads:
        load.start()

    held = counts_ref[group]

    def chosen(target, room):
        pick = jnp.int32(0)
        seen = jnp.int32(0)
        for q in range(slots):
            hit = jnp.logical_and(q < held, dest_ref[group, q] // NFD == target)
            pick = jnp.where(jnp.logical_and(hit, seen == room), jnp.int32(q), pick)
            seen = seen + hit.astype(jnp.int32)
        return pick

    def dp_copy(t):
        target = lax.rem(group + 2 * groups - 1 - lax.rem(t, groups), groups)
        return pltpu.make_async_remote_copy(
            src_ref=send.at[t], dst_ref=arr.at[t],
            send_sem=dp_send.at[t], recv_sem=dp_recv.at[t],
            device_id=(target, shard), device_id_type=MESH,
        )

    def pack(room):
        def body(j, c):
            t = room * groups + j
            target = lax.rem(group + groups - 1 - j, groups)
            send[t] = tok_ref[chosen(target, room)]
            return c
        return body

    def start_dp(room):
        def body(j, c):
            dp_copy(room * groups + j).start()
            return c
        return body

    lax.fori_loop(0, groups, pack(0), 0)
    pl.semaphore_wait(barrier, groups + shards - 2)
    lax.fori_loop(0, groups - 1, start_dp(0), 0)
    for room in range(1, rooms):
        lax.fori_loop(0, groups, pack(room), 0)
        lax.fori_loop(0, groups - 1, start_dp(room), 0)
    for room in range(rooms):
        own = room * groups + groups - 1
        arr[own] = send[own]

    loads[0].wait()
    loads[1].wait()

    def seq_copy(b, i):
        peer = lax.rem(shard + 1 + i, shards)
        return pltpu.make_async_remote_copy(
            src_ref=arr.at[pl.ds(b * BATCH, BATCH), peer],
            dst_ref=arr2.at[shard, pl.ds(b * BATCH, BATCH)],
            send_sem=sq_send.at[b, i], recv_sem=sq_recv.at[b, i],
            device_id=(group, peer), device_id_type=MESH,
        )

    tall = BATCH * patches
    frame_of = lax.broadcasted_iota(jnp.int32, (tall, tall), 0) // patches
    same_frame = frame_of == lax.broadcasted_iota(jnp.int32, (tall, tall), 1) // patches

    def spatial(b, c):
        for n in range(BATCH):
            t = b * BATCH + n

            @pl.when(lax.rem(t, groups) != groups - 1)
            def _():
                dp_copy(t).wait_recv()

        x = arr[pl.ds(b * BATCH, BATCH)].astype(jnp.float32).reshape(tall, width)
        normed = norm_mod(x, mod_ref[0:1, :], mod_ref[1:2, :])
        qkv = jnp.dot(normed, wqs[...], preferred_element_type=jnp.float32).astype(jnp.bfloat16)
        mixed = attend(qkv, same_frame).astype(jnp.bfloat16)
        projected = jnp.dot(mixed, wos[...], preferred_element_type=jnp.float32)
        y = x + mod_ref[2:3, :] * projected
        arr[pl.ds(b * BATCH, BATCH)] = y.reshape(BATCH, shards, widest, width).astype(jnp.bfloat16)
        for i in range(shards - 1):
            seq_copy(b, i).start()
        arr2[shard, pl.ds(b * BATCH, BATCH)] = arr[pl.ds(b * BATCH, BATCH), shard]
        return c

    lax.fori_loop(0, batches, spatial, 0)

    def find(source, found):
        found = list(found)
        live = counts_ref[source]
        seen = jnp.int32(0)
        offset = lax.rem(source + groups - 1 - group + groups, groups)
        for q in range(slots):
            place = dest_ref[source, q] - group * NFD
            hit = jnp.logical_and(q < live, jnp.logical_and(place >= 0, place < NFD))
            code = seen * groups + offset
            for k in range(NFD):
                found[k] = jnp.where(jnp.logical_and(hit, place == k), code, found[k])
            seen = seen + hit.astype(jnp.int32)
        return tuple(found)

    found = lax.fori_loop(0, groups, find, (jnp.int32(0),) * NFD)

    loads[2].wait()
    loads[3].wait()

    def arrived(b, c):
        for i in range(shards - 1):
            seq_copy(b, i).wait_recv()
        return c

    lax.fori_loop(0, batches, arrived, 0)

    for k in range(NFD):
        for s in range(shards):
            rows[k * shards + s] = arr2[s, found[k]]

    halves = widest // HALF
    part = frames * HALF
    x = rows[...].astype(jnp.float32)
    patch_of = lax.rem(lax.broadcasted_iota(jnp.int32, (part, part), 0), HALF)
    same_patch = patch_of == lax.rem(lax.broadcasted_iota(jnp.int32, (part, part), 1), HALF)
    flat = x.reshape(frames * widest, width)
    normed = norm_mod(flat, mod_ref[3:4, :], mod_ref[4:5, :])
    qkv = jnp.dot(normed, wqt[...], preferred_element_type=jnp.float32)
    qkv = qkv.reshape(frames, widest, qkv.shape[-1])
    mixed = []
    for n in range(halves):
        piece = qkv[:, n * HALF : (n + 1) * HALF, :].reshape(part, qkv.shape[-1]).astype(jnp.bfloat16)
        mixed.append(attend(piece, same_patch).reshape(frames, HALF, HEADS * HEAD_DIM))
    mixed = jnp.concatenate(mixed, axis=1).reshape(frames * widest, HEADS * HEAD_DIM).astype(jnp.bfloat16)
    projected = jnp.dot(mixed, wot[...], preferred_element_type=jnp.float32)
    y = (flat + mod_ref[5:6, :] * projected).reshape(frames, widest, width).astype(jnp.bfloat16)
    for k in range(NFD):
        for s in range(shards):
            res[s, k] = y[k * shards + s]

    def home_copy(i):
        peer = lax.rem(shard + 1 + i, shards)
        return pltpu.make_async_remote_copy(
            src_ref=res.at[peer], dst_ref=out_ref.at[:, shard],
            send_sem=home_send.at[i], recv_sem=home_recv.at[i],
            device_id=(group, peer), device_id_type=MESH,
        )

    for i in range(shards - 1):
        home_copy(i).start()
    out_ref[:, shard] = res[shard]

    for room in range(rooms):
        def sent(j, c):
            dp_copy(room * groups + j).wait_send()
            return c
        lax.fori_loop(0, groups - 1, sent, 0)

    def sent_seq(b, c):
        for i in range(shards - 1):
            seq_copy(b, i).wait_send()
        return c

    lax.fori_loop(0, batches, sent_seq, 0)
    for i in range(shards - 1):
        home_copy(i).wait()


def solution(mesh):
    groups, shards = mesh.shape["dp"], mesh.shape["seq"]

    def on_device(tokens, modulation, counts, dest, wqs, wos, wqt, wot):
        slots, patches, width = tokens.shape
        rooms = (slots + groups - 1) // groups
        widest = patches // shards
        total = rooms * groups
        bf = jnp.bfloat16
        vmem = pl.BlockSpec(memory_space=pltpu.VMEM)
        smem = pl.BlockSpec(memory_space=pltpu.SMEM)
        hbm = pl.BlockSpec(memory_space=pl.ANY)
        dma = pltpu.SemaphoreType.DMA
        out = pl.pallas_call(
            functools.partial(kernel, groups, shards, rooms),
            out_shape=jax.ShapeDtypeStruct((NFD, shards, widest, width), bf),
            in_specs=[smem, smem, vmem, vmem, hbm, hbm, hbm, hbm],
            out_specs=vmem,
            scratch_shapes=[
                pltpu.VMEM(wqs.shape, bf),
                pltpu.VMEM(wos.shape, bf),
                pltpu.VMEM(wqt.shape, bf),
                pltpu.VMEM(wot.shape, bf),
                pltpu.VMEM((total, shards, widest, width), bf),
                pltpu.VMEM((total, shards, widest, width), bf),
                pltpu.VMEM((shards, total, widest, width), bf),
                pltpu.VMEM((NFD * shards, widest, width), bf),
                pltpu.VMEM((shards, NFD, widest, width), bf),
                dma((4,)),
                dma((total,)),
                dma((total,)),
                dma((total // BATCH, shards - 1)),
                dma((total // BATCH, shards - 1)),
                dma((shards - 1,)),
                dma((shards - 1,)),
            ],
            compiler_params=pltpu.CompilerParams(
                collective_id=0, has_side_effects=True, vmem_limit_bytes=60 * 1024 * 1024
            ),
        )(counts, dest, tokens.reshape(slots, shards, widest, width), modulation[0], wqs, wos, wqt, wot)
        return out.reshape(NFD, patches, width)

    in_specs = (P("dp", "seq", None), P("dp", None, None), P(), P(), P(), P(), P(), P())
    return jax.shard_map(
        on_device, mesh=mesh, in_specs=in_specs, out_specs=P("dp", "seq", None), check_vma=False
    )
```

```python
import functools
import math

import jax
import jax.numpy as jnp
from jax import lax
from jax.experimental import pallas as pl
from jax.experimental.pallas import tpu as pltpu
from jax.sharding import PartitionSpec as P

HEADS = 8
HEAD_DIM = 72
NFD = 7
EPSILON = 1e-06
BATCH = 4
HALF = 8
MESH = pl.DeviceIdType.MESH


def norm_mod(values, shift_row, scale_row):
    center = values - jnp.mean(values, axis=-1, keepdims=True)
    spread = jnp.mean(center * center, axis=-1, keepdims=True)
    return (center * lax.rsqrt(spread + EPSILON) * (1.0 + scale_row) + shift_row).astype(jnp.bfloat16)


def flip(a, b, size):
    total, unit = 0, 1
    while unit < size:
        total = total + lax.rem(lax.rem(a // unit, 2) + lax.rem(b // unit, 2), 2) * unit
        unit *= 2
    return total


def project(rows, weight_t):
    return lax.dot_general(
        rows, weight_t[...], (((1,), (1,)), ((), ())), preferred_element_type=jnp.float32
    )


def attend(queries, qkv, same):
    width = HEADS * HEAD_DIM
    factor = 1.0 / math.sqrt(HEAD_DIM)
    mixed = []
    for head in range(HEADS):
        at = head * HEAD_DIM
        q = queries[:, at : at + HEAD_DIM]
        k = qkv[:, width + at : width + at + HEAD_DIM]
        v = qkv[:, 2 * width + at : 2 * width + at + HEAD_DIM]
        scores = lax.dot_general(q, k, (((1,), (1,)), ((), ())), preferred_element_type=jnp.float32)
        scores = jnp.where(same, scores * factor, -1e30)
        raised = jnp.exp(scores - jnp.max(scores, axis=-1, keepdims=True))
        weights = (raised * (1.0 / jnp.sum(raised, axis=-1, keepdims=True))).astype(jnp.bfloat16)
        mixed.append(jnp.dot(weights, v, preferred_element_type=jnp.float32))
    return jnp.concatenate(mixed, axis=-1)


def kernel(
    groups, shards, rooms,
    counts_ref, dest_ref, tok_ref, mod_ref, wqs_hbm, wos_hbm, wqt_hbm, wot_hbm,
    out_ref,
    wqs, wos, wqt, wot, send, arr, arr2, rows, res,
    w_sem, dp_send, dp_recv, sq_send, sq_recv, home_send, home_recv,
):
    group = lax.axis_index("dp")
    shard = lax.axis_index("seq")
    slots = tok_ref.shape[0]
    widest, width = tok_ref.shape[2], tok_ref.shape[3]
    patches = shards * widest
    room_slots = rooms * groups
    batches = room_slots // BATCH
    frames = NFD * shards

    barrier = pltpu.get_barrier_semaphore()

    def greet_dp(j, c):
        pl.semaphore_signal(
            barrier, inc=1, device_id=(flip(group, 1 + j, groups), shard), device_id_type=MESH
        )
        return c

    def greet_seq(i, c):
        pl.semaphore_signal(
            barrier, inc=1, device_id=(group, flip(shard, 1 + i, shards)), device_id_type=MESH
        )
        return c

    lax.fori_loop(0, groups - 1, greet_dp, 0)
    lax.fori_loop(0, shards - 1, greet_seq, 0)

    loads = [
        pltpu.make_async_copy(src, dst, w_sem.at[i])
        for i, (src, dst) in enumerate(
            ((wqs_hbm, wqs), (wos_hbm, wos), (wqt_hbm, wqt), (wot_hbm, wot))
        )
    ]
    for load in loads:
        load.start()

    held = counts_ref[group]

    def chosen(target, room):
        pick = jnp.int32(0)
        seen = jnp.int32(0)
        for q in range(slots):
            hit = jnp.logical_and(q < held, dest_ref[group, q] // NFD == target)
            pick = jnp.where(jnp.logical_and(hit, seen == room), jnp.int32(q), pick)
            seen = seen + hit.astype(jnp.int32)
        return pick

    def partner(i):
        near = lax.rem(i // 2 + 1, groups // 2)
        return flip(group, jnp.where(lax.rem(i, 2) == 0, groups // 2 + i // 2, near), groups)

    def dp_copy(t):
        target = partner(lax.rem(t, groups))
        return pltpu.make_async_remote_copy(
            src_ref=send.at[t], dst_ref=arr.at[t],
            send_sem=dp_send.at[t], recv_sem=dp_recv.at[t],
            device_id=(target, shard), device_id_type=MESH,
        )

    def pack(room):
        def body(j, c):
            t = room * groups + j
            send[t] = tok_ref[chosen(partner(j), room)]
            return c
        return body

    def start_dp(room):
        def body(j, c):
            dp_copy(room * groups + j).start()
            return c
        return body

    lax.fori_loop(0, groups, pack(0), 0)
    pl.semaphore_wait(barrier, groups + shards - 2)
    lax.fori_loop(0, groups - 1, start_dp(0), 0)
    for room in range(1, rooms):
        lax.fori_loop(0, groups, pack(room), 0)
        lax.fori_loop(0, groups - 1, start_dp(room), 0)
    for room in range(rooms):
        own = room * groups + groups - 1
        arr[own] = send[own]

    loads[0].wait()
    loads[1].wait()

    parts = [(b * BATCH, BATCH) for b in range(batches - 1)]
    parts += [((batches - 1) * BATCH + n * BATCH // 2, BATCH // 2) for n in range(2)]

    def seq_copy(b, first, size, x):
        peer = flip(shard, x, shards)
        return pltpu.make_async_remote_copy(
            src_ref=arr.at[pl.ds(first, size), peer],
            dst_ref=arr2.at[x, pl.ds(first, size)],
            send_sem=sq_send.at[b, x - 1], recv_sem=sq_recv.at[b, x - 1],
            device_id=(group, peer), device_id_type=MESH,
        )

    def same_frame(tall):
        frame_of = lax.broadcasted_iota(jnp.int32, (tall, tall), 0) // patches
        return frame_of == lax.broadcasted_iota(jnp.int32, (tall, tall), 1) // patches

    def spatial(b, first, size):
        tall = size * patches
        for n in range(size):
            t = first + n

            @pl.when(lax.rem(t, groups) != groups - 1)
            def _():
                dp_copy(t).wait_recv()

        x = arr[pl.ds(first, size)].astype(jnp.float32).reshape(tall, width)
        normed = norm_mod(x, mod_ref[0], mod_ref[1])
        qkv = project(normed, wqs).astype(jnp.bfloat16)
        mixed = attend(qkv, qkv, same_frame(tall)).astype(jnp.bfloat16)
        projected = jnp.dot(mixed, wos[...], preferred_element_type=jnp.float32)
        y = x + mod_ref[2] * projected
        arr[pl.ds(first, size)] = y.reshape(size, shards, widest, width).astype(jnp.bfloat16)
        for x in range(shards - 1, 0, -1):
            seq_copy(b, first, size, x).start()
        arr2[0, pl.ds(first, size)] = arr[pl.ds(first, size), shard]

    def full(b, c):
        spatial(b, b * BATCH, BATCH)
        return c

    lax.fori_loop(0, batches - 1, full, 0)
    short = BATCH // 2

    def last(n, c):
        spatial(batches - 1 + n, (batches - 1) * BATCH + n * short, short)
        return c

    lax.fori_loop(0, 2, last, 0)

    def find(source, found):
        found = list(found)
        live = counts_ref[source]
        seen = jnp.int32(0)
        apart = flip(source, group, groups)
        near = 2 * lax.rem(apart + groups // 2 - 1, groups // 2) + 1
        offset = jnp.where(apart >= groups // 2, 2 * (apart - groups // 2), near)
        for q in range(slots):
            place = dest_ref[source, q] - group * NFD
            hit = jnp.logical_and(q < live, jnp.logical_and(place >= 0, place < NFD))
            code = seen * groups + offset
            for k in range(NFD):
                found[k] = jnp.where(jnp.logical_and(hit, place == k), code, found[k])
            seen = seen + hit.astype(jnp.int32)
        return tuple(found)

    found = lax.fori_loop(0, groups, find, (jnp.int32(0),) * NFD)

    loads[2].wait()
    loads[3].wait()

    for b, (first, size) in enumerate(parts):
        for x in range(1, shards):
            seq_copy(b, first, size, x).wait_recv()

    order = list(range(shards - 1, -1, -1))
    for place, x in enumerate(order):
        for k in range(NFD):
            rows[place * NFD + k] = arr2[x, found[k]]

    def home_copy(x):
        peer = flip(shard, x, shards)
        return pltpu.make_async_remote_copy(
            src_ref=res.at[x], dst_ref=out_ref.at[:, shard],
            send_sem=home_send.at[x - 1], recv_sem=home_recv.at[x - 1],
            device_id=(group, peer), device_id_type=MESH,
        )

    halves = widest // HALF
    pieces = 2
    some = frames // pieces
    part = frames * HALF
    tokens = rows[...].astype(jnp.float32).reshape(frames * widest, width)
    normed = norm_mod(tokens, mod_ref[3], mod_ref[4])
    qkv = project(normed, wqt).reshape(frames, widest, 3 * HEADS * HEAD_DIM)
    by_patch = [
        qkv[:, n * HALF : (n + 1) * HALF, :].reshape(part, qkv.shape[-1]).astype(jnp.bfloat16)
        for n in range(halves)
    ]
    patch_of = lax.rem(lax.broadcasted_iota(jnp.int32, (some * HALF, part), 0), HALF)
    same_patch = patch_of == lax.rem(
        lax.broadcasted_iota(jnp.int32, (some * HALF, part), 1), HALF
    )
    for piece in range(pieces):
        begin = piece * some
        mixed = [
            attend(rows_of[begin * HALF : (begin + some) * HALF], rows_of, same_patch).reshape(
                some, HALF, HEADS * HEAD_DIM
            )
            for rows_of in by_patch
        ]
        mixed = jnp.concatenate(mixed, axis=1).reshape(some * widest, HEADS * HEAD_DIM)
        projected = jnp.dot(mixed.astype(jnp.bfloat16), wot[...], preferred_element_type=jnp.float32)
        y = rows[pl.ds(begin, some)].astype(jnp.float32) + (mod_ref[5] * projected).reshape(
            some, widest, width
        )
        y = y.astype(jnp.bfloat16).reshape(shards // pieces, NFD, widest, width)
        for n in range(shards // pieces):
            x = order[piece * shards // pieces + n]
            if x:
                res[x] = y[n]
                home_copy(x).start()
            else:
                out_ref[:, shard] = y[n]

    for room in range(rooms):
        def sent(j, c):
            dp_copy(room * groups + j).wait_send()
            return c
        lax.fori_loop(0, groups - 1, sent, 0)

    for b, (first, size) in enumerate(parts):
        for x in range(1, shards):
            seq_copy(b, first, size, x).wait_send()
    for x in range(1, shards):
        home_copy(x).wait()


def solution(mesh):
    groups, shards = mesh.shape["dp"], mesh.shape["seq"]

    def on_device(tokens, modulation, counts, dest, wqs, wos, wqt, wot):
        slots, patches, width = tokens.shape
        rooms = (slots + groups - 1) // groups
        widest = patches // shards
        total = rooms * groups
        bf = jnp.bfloat16
        vmem = pl.BlockSpec(memory_space=pltpu.VMEM)
        smem = pl.BlockSpec(memory_space=pltpu.SMEM)
        hbm = pl.BlockSpec(memory_space=pl.ANY)
        dma = pltpu.SemaphoreType.DMA
        out = pl.pallas_call(
            functools.partial(kernel, groups, shards, rooms),
            out_shape=jax.ShapeDtypeStruct((NFD, shards, widest, width), bf),
            in_specs=[smem, smem, vmem, vmem, hbm, hbm, hbm, hbm],
            out_specs=vmem,
            scratch_shapes=[
                pltpu.VMEM(wqs.shape[::-1], bf),
                pltpu.VMEM(wos.shape, bf),
                pltpu.VMEM(wqt.shape[::-1], bf),
                pltpu.VMEM(wot.shape, bf),
                pltpu.VMEM((total, shards, widest, width), bf),
                pltpu.VMEM((total, shards, widest, width), bf),
                pltpu.VMEM((shards, total, widest, width), bf),
                pltpu.VMEM((NFD * shards, widest, width), bf),
                pltpu.VMEM((shards, NFD, widest, width), bf),
                dma((4,)),
                dma((total,)),
                dma((total,)),
                dma((total // BATCH + 1, shards - 1)),
                dma((total // BATCH + 1, shards - 1)),
                dma((shards - 1,)),
                dma((shards - 1,)),
            ],
            compiler_params=pltpu.CompilerParams(
                collective_id=0, has_side_effects=True, vmem_limit_bytes=60 * 1024 * 1024
            ),
        )(
            counts, dest, tokens.reshape(slots, shards, widest, width),
            modulation.transpose(1, 0, 2), wqs.T, wos, wqt.T, wot,
        )
        return out.reshape(NFD, patches, width)

    in_specs = (P("dp", "seq", None), P("dp", None, None), P(), P(), P(), P(), P(), P())
    return jax.shard_map(
        on_device, mesh=mesh, in_specs=in_specs, out_specs=P("dp", "seq", None), check_vma=False
    )
```

```python
import functools
import math

import jax
import jax.numpy as jnp
from jax import lax
from jax.experimental import pallas as pl
from jax.experimental.pallas import tpu as pltpu
from jax.sharding import PartitionSpec as P

HEADS = 8
HEAD_DIM = 72
NFD = 7
EPSILON = 1e-06
BATCH = 4
HALF = 8
MESH = pl.DeviceIdType.MESH


def norm_mod(values, shift_row, scale_row):
    center = values - jnp.mean(values, axis=-1, keepdims=True)
    spread = jnp.mean(center * center, axis=-1, keepdims=True)
    return (center * lax.rsqrt(spread + EPSILON) * (1.0 + scale_row) + shift_row).astype(jnp.bfloat16)


def flip(a, b, size):
    total, unit = 0, 1
    while unit < size:
        total = total + lax.rem(lax.rem(a // unit, 2) + lax.rem(b // unit, 2), 2) * unit
        unit *= 2
    return total


def project(rows, weight_t):
    return lax.dot_general(
        rows, weight_t[...], (((1,), (1,)), ((), ())), preferred_element_type=jnp.float32
    )


def attend(queries, qkv, same):
    width = HEADS * HEAD_DIM
    factor = 1.0 / math.sqrt(HEAD_DIM)
    mixed = []
    for head in range(HEADS):
        at = head * HEAD_DIM
        q = queries[:, at : at + HEAD_DIM]
        k = qkv[:, width + at : width + at + HEAD_DIM]
        v = qkv[:, 2 * width + at : 2 * width + at + HEAD_DIM]
        scores = lax.dot_general(q, k, (((1,), (1,)), ((), ())), preferred_element_type=jnp.float32)
        scores = jnp.where(same, scores * factor, -1e30)
        raised = jnp.exp(scores - jnp.max(scores, axis=-1, keepdims=True))
        weights = (raised * (1.0 / jnp.sum(raised, axis=-1, keepdims=True))).astype(jnp.bfloat16)
        mixed.append(jnp.dot(weights, v, preferred_element_type=jnp.float32))
    return jnp.concatenate(mixed, axis=-1)


def kernel(
    groups, shards, rooms, extra_count,
    counts_ref, dest_ref, tok_ref, mod_ref, wqs_hbm, wos_hbm, wqt_hbm, wot_hbm,
    out_ref,
    wqs, wos, wqt, wot, send, arr, over, arr2, qkv2, rows, qkv_rows, res,
    w_sem, dp_send, dp_recv, sq_send, sq_recv, home_send, home_recv,
):
    group = lax.axis_index("dp")
    shard = lax.axis_index("seq")
    slots = tok_ref.shape[0]
    widest, width = tok_ref.shape[2], tok_ref.shape[3]
    patches = shards * widest
    batches = groups // BATCH
    frames = NFD * shards

    barrier = pltpu.get_barrier_semaphore()

    def greet_dp(j, c):
        pl.semaphore_signal(
            barrier, inc=1, device_id=(flip(group, 1 + j, groups), shard), device_id_type=MESH
        )
        return c

    def greet_seq(i, c):
        pl.semaphore_signal(
            barrier, inc=1, device_id=(group, flip(shard, 1 + i, shards)), device_id_type=MESH
        )
        return c

    lax.fori_loop(0, groups - 1, greet_dp, 0)
    lax.fori_loop(0, shards - 1, greet_seq, 0)

    loads = [
        pltpu.make_async_copy(src, dst, w_sem.at[i])
        for i, (src, dst) in enumerate(
            ((wqs_hbm, wqs), (wos_hbm, wos), (wqt_hbm, wqt), (wot_hbm, wot))
        )
    ]
    for load in loads:
        load.start()

    held = counts_ref[group]

    def chosen(target, room):
        pick = jnp.int32(0)
        seen = jnp.int32(0)
        for q in range(slots):
            hit = jnp.logical_and(q < held, dest_ref[group, q] // NFD == target)
            pick = jnp.where(jnp.logical_and(hit, seen == room), jnp.int32(q), pick)
            seen = seen + hit.astype(jnp.int32)
        return pick

    def partner(i):
        near = lax.rem(i // 2 + 1, groups // 2)
        return flip(group, jnp.where(lax.rem(i, 2) == 0, groups // 2 + i // 2, near), groups)

    def dp_copy(t):
        target = partner(lax.rem(t, groups))
        return pltpu.make_async_remote_copy(
            src_ref=send.at[t], dst_ref=arr.at[t],
            send_sem=dp_send.at[t], recv_sem=dp_recv.at[t],
            device_id=(target, shard), device_id_type=MESH,
        )

    def pack(room):
        def body(j, c):
            t = room * groups + j
            send[t] = tok_ref[chosen(partner(j), room)]
            return c
        return body

    def start_dp(room):
        def body(j, c):
            dp_copy(room * groups + j).start()
            return c
        return body

    lax.fori_loop(0, groups, pack(0), 0)
    pl.semaphore_wait(barrier, groups + shards - 2)
    lax.fori_loop(0, groups - 1, start_dp(0), 0)
    for room in range(1, rooms):
        lax.fori_loop(0, groups, pack(room), 0)
        lax.fori_loop(0, groups - 1, start_dp(room), 0)
    for room in range(rooms):
        own = room * groups + groups - 1
        arr[own] = send[own]

    loads[0].wait()
    loads[1].wait()

    parts = [(b * BATCH, BATCH) for b in range(batches)]
    if extra_count:
        parts.append((groups, extra_count))

    def seq_copy(b, src, first, size, x):
        peer = flip(shard, x, shards)
        return pltpu.make_async_remote_copy(
            src_ref=src.at[:, peer] if src is over else src.at[pl.ds(first, size), peer],
            dst_ref=arr2.at[x, pl.ds(first, size)],
            send_sem=sq_send.at[b, x - 1], recv_sem=sq_recv.at[b, x - 1],
            device_id=(group, peer), device_id_type=MESH,
        )

    def same_frame(tall):
        frame_of = lax.broadcasted_iota(jnp.int32, (tall, tall), 0) // patches
        return frame_of == lax.broadcasted_iota(jnp.int32, (tall, tall), 1) // patches

    def spatial(values, size):
        tall = size * patches
        tokens = values.astype(jnp.float32).reshape(tall, width)
        normed = norm_mod(tokens, mod_ref[0], mod_ref[1])
        qkv = project(normed, wqs).astype(jnp.bfloat16)
        mixed = attend(qkv, qkv, same_frame(tall)).astype(jnp.bfloat16)
        projected = jnp.dot(mixed, wos[...], preferred_element_type=jnp.float32)
        y = tokens + mod_ref[2] * projected
        return y.reshape(size, shards, widest, width).astype(jnp.bfloat16)

    def full(b, c):
        for n in range(BATCH):
            t = b * BATCH + n

            @pl.when(t != groups - 1)
            def _():
                dp_copy(t).wait_recv()

        at = pl.ds(b * BATCH, BATCH)
        arr[at] = spatial(arr[at], BATCH)
        for x in range(shards - 1, 0, -1):
            seq_copy(b, arr, b * BATCH, BATCH, x).start()
        arr2[0, at] = arr[at, shard]
        return c

    lax.fori_loop(0, batches, full, 0)

    loads[2].wait()
    loads[3].wait()

    def prepare(b, src, first, size):
        for x in range(1, shards):
            seq_copy(b, src, first, size, x).wait_recv()
        tokens = arr2[:, pl.ds(first, size)].astype(jnp.float32).reshape(-1, width)
        qkv = project(norm_mod(tokens, mod_ref[3], mod_ref[4]), wqt)
        qkv2[:, pl.ds(first, size)] = qkv.reshape(
            shards, size, widest, qkv.shape[-1]
        ).astype(jnp.bfloat16)

    def prepare_full(b, c):
        prepare(b, arr, b * BATCH, BATCH)
        return c

    lax.fori_loop(0, batches, prepare_full, 0)

    def find(source, state):
        found, extra, taken = list(state[0]), list(state[1]), state[2]
        live = counts_ref[source]
        seen = jnp.int32(0)
        apart = flip(source, group, groups)
        near = 2 * lax.rem(apart + groups // 2 - 1, groups // 2) + 1
        offset = jnp.where(apart >= groups // 2, 2 * (apart - groups // 2), near)
        for q in range(slots):
            place = dest_ref[source, q] - group * NFD
            hit = jnp.logical_and(q < live, jnp.logical_and(place >= 0, place < NFD))
            second = jnp.logical_and(hit, seen >= 1)
            code = jnp.where(second, groups + taken, offset)
            for k in range(NFD):
                found[k] = jnp.where(jnp.logical_and(hit, place == k), code, found[k])
            for e in range(extra_count):
                extra[e] = jnp.where(
                    jnp.logical_and(second, taken == e), seen * groups + offset, extra[e]
                )
            taken = taken + second.astype(jnp.int32)
            seen = seen + hit.astype(jnp.int32)
        return tuple(found), tuple(extra), taken

    zero = jnp.int32(0)
    found, extra, _ = lax.fori_loop(
        0, groups, find, ((zero,) * NFD, (zero,) * extra_count, zero)
    )

    if extra_count:
        for room in range(1, rooms):
            def come(j, c):
                dp_copy(room * groups + j).wait_recv()
                return c
            lax.fori_loop(0, groups - 1, come, 0)
        for e in range(extra_count):
            over[e] = arr[extra[e]]
        over[...] = spatial(over[...], extra_count)
        for x in range(shards - 1, 0, -1):
            seq_copy(batches, over, groups, extra_count, x).start()
        arr2[0, pl.ds(groups, extra_count)] = over[:, shard]
        prepare(batches, over, groups, extra_count)

    order = list(range(shards - 1, -1, -1))
    for place, x in enumerate(order):
        for k in range(NFD):
            rows[place * NFD + k] = arr2[x, found[k]]
            qkv_rows[place * NFD + k] = qkv2[x, found[k]]

    def home_copy(x):
        peer = flip(shard, x, shards)
        return pltpu.make_async_remote_copy(
            src_ref=res.at[x], dst_ref=out_ref.at[:, shard],
            send_sem=home_send.at[x - 1], recv_sem=home_recv.at[x - 1],
            device_id=(group, peer), device_id_type=MESH,
        )

    halves = widest // HALF
    pieces = 2
    some = frames // pieces
    part = frames * HALF
    qkv = qkv_rows[...].astype(jnp.float32)
    by_patch = [
        qkv[:, n * HALF : (n + 1) * HALF, :].reshape(part, qkv.shape[-1]).astype(jnp.bfloat16)
        for n in range(halves)
    ]
    patch_of = lax.rem(lax.broadcasted_iota(jnp.int32, (some * HALF, part), 0), HALF)
    same_patch = patch_of == lax.rem(
        lax.broadcasted_iota(jnp.int32, (some * HALF, part), 1), HALF
    )
    for piece in range(pieces):
        begin = piece * some
        mixed = [
            attend(rows_of[begin * HALF : (begin + some) * HALF], rows_of, same_patch).reshape(
                some, HALF, HEADS * HEAD_DIM
            )
            for rows_of in by_patch
        ]
        mixed = jnp.concatenate(mixed, axis=1).reshape(some * widest, HEADS * HEAD_DIM)
        projected = jnp.dot(mixed.astype(jnp.bfloat16), wot[...], preferred_element_type=jnp.float32)
        y = rows[pl.ds(begin, some)].astype(jnp.float32) + (mod_ref[5] * projected).reshape(
            some, widest, width
        )
        y = y.astype(jnp.bfloat16).reshape(shards // pieces, NFD, widest, width)
        for n in range(shards // pieces):
            x = order[piece * shards // pieces + n]
            if x:
                res[x] = y[n]
                home_copy(x).start()
            else:
                out_ref[:, shard] = y[n]

    for room in range(rooms):
        def sent(j, c):
            dp_copy(room * groups + j).wait_send()
            return c
        lax.fori_loop(0, groups - 1, sent, 0)

    for b, (first, size) in enumerate(parts):
        for x in range(1, shards):
            seq_copy(b, over if first == groups else arr, first, size, x).wait_send()
    for x in range(1, shards):
        home_copy(x).wait()


def solution(mesh):
    groups, shards = mesh.shape["dp"], mesh.shape["seq"]

    def on_device(tokens, modulation, counts, dest, wqs, wos, wqt, wot):
        slots, patches, width = tokens.shape
        rooms = (slots + groups - 1) // groups
        widest = patches // shards
        total = rooms * groups
        extras = NFD * (rooms - 1) // rooms
        kinds = wqs.shape[-1]
        bf = jnp.bfloat16
        vmem = pl.BlockSpec(memory_space=pltpu.VMEM)
        smem = pl.BlockSpec(memory_space=pltpu.SMEM)
        hbm = pl.BlockSpec(memory_space=pl.ANY)
        dma = pltpu.SemaphoreType.DMA
        out = pl.pallas_call(
            functools.partial(kernel, groups, shards, rooms, extras),
            out_shape=jax.ShapeDtypeStruct((NFD, shards, widest, width), bf),
            in_specs=[smem, smem, vmem, vmem, hbm, hbm, hbm, hbm],
            out_specs=vmem,
            scratch_shapes=[
                pltpu.VMEM(wqs.shape[::-1], bf),
                pltpu.VMEM(wos.shape, bf),
                pltpu.VMEM(wqt.shape[::-1], bf),
                pltpu.VMEM(wot.shape, bf),
                pltpu.VMEM((total, shards, widest, width), bf),
                pltpu.VMEM((total, shards, widest, width), bf),
                pltpu.VMEM((max(extras, 1), shards, widest, width), bf),
                pltpu.VMEM((shards, groups + extras, widest, width), bf),
                pltpu.VMEM((shards, groups + extras, widest, kinds), bf),
                pltpu.VMEM((NFD * shards, widest, width), bf),
                pltpu.VMEM((NFD * shards, widest, kinds), bf),
                pltpu.VMEM((shards, NFD, widest, width), bf),
                dma((4,)),
                dma((total,)),
                dma((total,)),
                dma((groups // BATCH + 1, shards - 1)),
                dma((groups // BATCH + 1, shards - 1)),
                dma((shards - 1,)),
                dma((shards - 1,)),
            ],
            compiler_params=pltpu.CompilerParams(
                collective_id=0, has_side_effects=True, vmem_limit_bytes=60 * 1024 * 1024
            ),
        )(
            counts, dest, tokens.reshape(slots, shards, widest, width),
            modulation.transpose(1, 0, 2), wqs.T, wos, wqt.T, wot,
        )
        return out.reshape(NFD, patches, width)

    in_specs = (P("dp", "seq", None), P("dp", None, None), P(), P(), P(), P(), P(), P())
    return jax.shard_map(
        on_device, mesh=mesh, in_specs=in_specs, out_specs=P("dp", "seq", None), check_vma=False
    )
```

```python
import functools
import math

import jax
import jax.numpy as jnp
from jax import lax
from jax.experimental import pallas as pl
from jax.experimental.pallas import tpu as pltpu
from jax.sharding import PartitionSpec as P

HEADS = 8
HEAD_DIM = 72
NFD = 7
EPSILON = 1e-06
BATCH = 4
HALF = 8
MESH = pl.DeviceIdType.MESH


def norm_mod(values, shift_row, scale_row):
    center = values - jnp.mean(values, axis=-1, keepdims=True)
    spread = jnp.mean(center * center, axis=-1, keepdims=True)
    return (center * lax.rsqrt(spread + EPSILON) * (1.0 + scale_row) + shift_row).astype(jnp.bfloat16)


def flip(a, b, size):
    total, unit = 0, 1
    while unit < size:
        total = total + lax.rem(lax.rem(a // unit, 2) + lax.rem(b // unit, 2), 2) * unit
        unit *= 2
    return total


def project(rows, weight_t):
    return lax.dot_general(
        rows, weight_t[...], (((1,), (1,)), ((), ())), preferred_element_type=jnp.float32
    )


def attend(queries, qkv, same):
    width = HEADS * HEAD_DIM
    factor = 1.0 / math.sqrt(HEAD_DIM)
    mixed = []
    for head in range(HEADS):
        at = head * HEAD_DIM
        q = queries[:, at : at + HEAD_DIM]
        k = qkv[:, width + at : width + at + HEAD_DIM]
        v = qkv[:, 2 * width + at : 2 * width + at + HEAD_DIM]
        scores = lax.dot_general(q, k, (((1,), (1,)), ((), ())), preferred_element_type=jnp.float32)
        scores = jnp.where(same, scores * factor, -1e30)
        raised = jnp.exp(scores - jnp.max(scores, axis=-1, keepdims=True))
        weights = (raised * (1.0 / jnp.sum(raised, axis=-1, keepdims=True))).astype(jnp.bfloat16)
        mixed.append(jnp.dot(weights, v, preferred_element_type=jnp.float32))
    return jnp.concatenate(mixed, axis=-1)


def kernel(
    groups, shards, rooms, extra_count,
    counts_ref, dest_ref, tok_ref, mod_ref, wqs_hbm, wos_hbm, wqt_hbm, wot_hbm,
    out_ref,
    wqs, wos, wqt, wot, send, arr, over, arr2, qkv2, rows, qkv_rows, res,
    w_sem, dp_send, dp_recv, sq_send, sq_recv, home_send, home_recv,
):
    group = lax.axis_index("dp")
    shard = lax.axis_index("seq")
    slots = tok_ref.shape[0]
    widest, width = tok_ref.shape[2], tok_ref.shape[3]
    patches = shards * widest
    batches = groups // BATCH
    frames = NFD * shards

    barrier = pltpu.get_barrier_semaphore()

    def greet_dp(j, c):
        pl.semaphore_signal(
            barrier, inc=1, device_id=(flip(group, 1 + j, groups), shard), device_id_type=MESH
        )
        return c

    def greet_seq(i, c):
        pl.semaphore_signal(
            barrier, inc=1, device_id=(group, flip(shard, 1 + i, shards)), device_id_type=MESH
        )
        return c

    lax.fori_loop(0, groups - 1, greet_dp, 0)
    lax.fori_loop(0, shards - 1, greet_seq, 0)

    loads = [
        pltpu.make_async_copy(src, dst, w_sem.at[i])
        for i, (src, dst) in enumerate(
            ((wqs_hbm, wqs), (wos_hbm, wos), (wqt_hbm, wqt), (wot_hbm, wot))
        )
    ]
    for load in loads:
        load.start()

    held = counts_ref[group]

    def chosen(target, room):
        pick = jnp.int32(0)
        seen = jnp.int32(0)
        for q in range(slots):
            hit = jnp.logical_and(q < held, dest_ref[group, q] // NFD == target)
            pick = jnp.where(jnp.logical_and(hit, seen == room), jnp.int32(q), pick)
            seen = seen + hit.astype(jnp.int32)
        return pick

    def partner(i):
        near = lax.rem(i // 2 + 1, groups // 2)
        return flip(group, jnp.where(lax.rem(i, 2) == 0, groups // 2 + i // 2, near), groups)

    def dp_copy(t):
        target = partner(lax.rem(t, groups))
        return pltpu.make_async_remote_copy(
            src_ref=send.at[t], dst_ref=arr.at[t],
            send_sem=dp_send.at[t], recv_sem=dp_recv.at[t],
            device_id=(target, shard), device_id_type=MESH,
        )

    def pack(room):
        def body(j, c):
            t = room * groups + j
            send[t] = tok_ref[chosen(partner(j), room)]
            return c
        return body

    def start_dp(room):
        def body(j, c):
            dp_copy(room * groups + j).start()
            return c
        return body

    lax.fori_loop(0, groups, pack(0), 0)
    pl.semaphore_wait(barrier, groups + shards - 2)
    lax.fori_loop(0, groups - 1, start_dp(0), 0)
    for room in range(1, rooms):
        lax.fori_loop(0, groups, pack(room), 0)
    for room in range(rooms):
        own = room * groups + groups - 1
        arr[own] = send[own]

    loads[0].wait()
    loads[1].wait()

    parts = [(b * BATCH, BATCH) for b in range(batches)]
    if extra_count:
        parts.append((groups, extra_count))

    def seq_copy(b, src, first, size, x):
        peer = flip(shard, x, shards)
        return pltpu.make_async_remote_copy(
            src_ref=src.at[:, peer] if src is over else src.at[pl.ds(first, size), peer],
            dst_ref=arr2.at[x, pl.ds(first, size)],
            send_sem=sq_send.at[b, x - 1], recv_sem=sq_recv.at[b, x - 1],
            device_id=(group, peer), device_id_type=MESH,
        )

    def same_frame(tall):
        frame_of = lax.broadcasted_iota(jnp.int32, (tall, tall), 0) // patches
        return frame_of == lax.broadcasted_iota(jnp.int32, (tall, tall), 1) // patches

    def spatial(values, size):
        tall = size * patches
        tokens = values.astype(jnp.float32).reshape(tall, width)
        normed = norm_mod(tokens, mod_ref[0], mod_ref[1])
        qkv = project(normed, wqs).astype(jnp.bfloat16)
        mixed = attend(qkv, qkv, same_frame(tall)).astype(jnp.bfloat16)
        projected = jnp.dot(mixed, wos[...], preferred_element_type=jnp.float32)
        y = tokens + mod_ref[2] * projected
        return y.reshape(size, shards, widest, width).astype(jnp.bfloat16)

    def full(b, c):
        for n in range(BATCH):
            t = b * BATCH + n

            @pl.when(t != groups - 1)
            def _():
                dp_copy(t).wait_recv()

        for n in range(BATCH):
            t = b * BATCH + n

            @pl.when(t != groups - 1)
            def _():
                for room in range(1, rooms):
                    dp_copy(room * groups + t).start()

        at = pl.ds(b * BATCH, BATCH)
        arr[at] = spatial(arr[at], BATCH)
        for x in range(shards - 1, 0, -1):
            seq_copy(b, arr, b * BATCH, BATCH, x).start()
        arr2[0, at] = arr[at, shard]
        return c

    lax.fori_loop(0, batches, full, 0)

    loads[2].wait()
    loads[3].wait()

    def prepare(b, src, first, size):
        for x in range(1, shards):
            seq_copy(b, src, first, size, x).wait_recv()
        tokens = arr2[:, pl.ds(first, size)].astype(jnp.float32).reshape(-1, width)
        qkv = project(norm_mod(tokens, mod_ref[3], mod_ref[4]), wqt)
        qkv2[:, pl.ds(first, size)] = qkv.reshape(
            shards, size, widest, qkv.shape[-1]
        ).astype(jnp.bfloat16)

    def prepare_full(b, c):
        prepare(b, arr, b * BATCH, BATCH)
        return c

    lax.fori_loop(0, batches, prepare_full, 0)

    def find(source, state):
        found, extra, taken = list(state[0]), list(state[1]), state[2]
        live = counts_ref[source]
        seen = jnp.int32(0)
        apart = flip(source, group, groups)
        near = 2 * lax.rem(apart + groups // 2 - 1, groups // 2) + 1
        offset = jnp.where(apart >= groups // 2, 2 * (apart - groups // 2), near)
        for q in range(slots):
            place = dest_ref[source, q] - group * NFD
            hit = jnp.logical_and(q < live, jnp.logical_and(place >= 0, place < NFD))
            second = jnp.logical_and(hit, seen >= 1)
            code = jnp.where(second, groups + taken, offset)
            for k in range(NFD):
                found[k] = jnp.where(jnp.logical_and(hit, place == k), code, found[k])
            for e in range(extra_count):
                extra[e] = jnp.where(
                    jnp.logical_and(second, taken == e), seen * groups + offset, extra[e]
                )
            taken = taken + second.astype(jnp.int32)
            seen = seen + hit.astype(jnp.int32)
        return tuple(found), tuple(extra), taken

    zero = jnp.int32(0)
    found, extra, _ = lax.fori_loop(
        0, groups, find, ((zero,) * NFD, (zero,) * extra_count, zero)
    )

    if extra_count:
        for room in range(1, rooms):
            def come(j, c):
                dp_copy(room * groups + j).wait_recv()
                return c
            lax.fori_loop(0, groups - 1, come, 0)
        for e in range(extra_count):
            over[e] = arr[extra[e]]
        over[...] = spatial(over[...], extra_count)
        for x in range(shards - 1, 0, -1):
            seq_copy(batches, over, groups, extra_count, x).start()
        arr2[0, pl.ds(groups, extra_count)] = over[:, shard]
        prepare(batches, over, groups, extra_count)

    order = list(range(shards - 1, -1, -1))
    for place, x in enumerate(order):
        for k in range(NFD):
            rows[place * NFD + k] = arr2[x, found[k]]
            qkv_rows[place * NFD + k] = qkv2[x, found[k]]

    def home_copy(x):
        peer = flip(shard, x, shards)
        return pltpu.make_async_remote_copy(
            src_ref=res.at[x], dst_ref=out_ref.at[:, shard],
            send_sem=home_send.at[x - 1], recv_sem=home_recv.at[x - 1],
            device_id=(group, peer), device_id_type=MESH,
        )

    halves = widest // HALF
    pieces = 2
    some = frames // pieces
    part = frames * HALF
    qkv = qkv_rows[...].astype(jnp.float32)
    by_patch = [
        qkv[:, n * HALF : (n + 1) * HALF, :].reshape(part, qkv.shape[-1]).astype(jnp.bfloat16)
        for n in range(halves)
    ]
    patch_of = lax.rem(lax.broadcasted_iota(jnp.int32, (some * HALF, part), 0), HALF)
    same_patch = patch_of == lax.rem(
        lax.broadcasted_iota(jnp.int32, (some * HALF, part), 1), HALF
    )
    for piece in range(pieces):
        begin = piece * some
        mixed = [
            attend(rows_of[begin * HALF : (begin + some) * HALF], rows_of, same_patch).reshape(
                some, HALF, HEADS * HEAD_DIM
            )
            for rows_of in by_patch
        ]
        mixed = jnp.concatenate(mixed, axis=1).reshape(some * widest, HEADS * HEAD_DIM)
        projected = jnp.dot(mixed.astype(jnp.bfloat16), wot[...], preferred_element_type=jnp.float32)
        y = rows[pl.ds(begin, some)].astype(jnp.float32) + (mod_ref[5] * projected).reshape(
            some, widest, width
        )
        y = y.astype(jnp.bfloat16).reshape(shards // pieces, NFD, widest, width)
        for n in range(shards // pieces):
            x = order[piece * shards // pieces + n]
            if x:
                res[x] = y[n]
                home_copy(x).start()
            else:
                out_ref[:, shard] = y[n]

    for room in range(rooms):
        def sent(j, c):
            dp_copy(room * groups + j).wait_send()
            return c
        lax.fori_loop(0, groups - 1, sent, 0)

    for b, (first, size) in enumerate(parts):
        for x in range(1, shards):
            seq_copy(b, over if first == groups else arr, first, size, x).wait_send()
    for x in range(1, shards):
        home_copy(x).wait()


def solution(mesh):
    groups, shards = mesh.shape["dp"], mesh.shape["seq"]

    def on_device(tokens, modulation, counts, dest, wqs, wos, wqt, wot):
        slots, patches, width = tokens.shape
        rooms = (slots + groups - 1) // groups
        widest = patches // shards
        total = rooms * groups
        extras = NFD * (rooms - 1) // rooms
        kinds = wqs.shape[-1]
        bf = jnp.bfloat16
        vmem = pl.BlockSpec(memory_space=pltpu.VMEM)
        smem = pl.BlockSpec(memory_space=pltpu.SMEM)
        hbm = pl.BlockSpec(memory_space=pl.ANY)
        dma = pltpu.SemaphoreType.DMA
        out = pl.pallas_call(
            functools.partial(kernel, groups, shards, rooms, extras),
            out_shape=jax.ShapeDtypeStruct((NFD, shards, widest, width), bf),
            in_specs=[smem, smem, vmem, vmem, hbm, hbm, hbm, hbm],
            out_specs=vmem,
            scratch_shapes=[
                pltpu.VMEM(wqs.shape[::-1], bf),
                pltpu.VMEM(wos.shape, bf),
                pltpu.VMEM(wqt.shape[::-1], bf),
                pltpu.VMEM(wot.shape, bf),
                pltpu.VMEM((total, shards, widest, width), bf),
                pltpu.VMEM((total, shards, widest, width), bf),
                pltpu.VMEM((max(extras, 1), shards, widest, width), bf),
                pltpu.VMEM((shards, groups + extras, widest, width), bf),
                pltpu.VMEM((shards, groups + extras, widest, kinds), bf),
                pltpu.VMEM((NFD * shards, widest, width), bf),
                pltpu.VMEM((NFD * shards, widest, kinds), bf),
                pltpu.VMEM((shards, NFD, widest, width), bf),
                dma((4,)),
                dma((total,)),
                dma((total,)),
                dma((groups // BATCH + 1, shards - 1)),
                dma((groups // BATCH + 1, shards - 1)),
                dma((shards - 1,)),
                dma((shards - 1,)),
            ],
            compiler_params=pltpu.CompilerParams(
                collective_id=0, has_side_effects=True, vmem_limit_bytes=60 * 1024 * 1024
            ),
        )(
            counts, dest, tokens.reshape(slots, shards, widest, width),
            modulation.transpose(1, 0, 2), wqs.T, wos, wqt.T, wot,
        )
        return out.reshape(NFD, patches, width)

    in_specs = (P("dp", "seq", None), P("dp", None, None), P(), P(), P(), P(), P(), P())
    return jax.shard_map(
        on_device, mesh=mesh, in_specs=in_specs, out_specs=P("dp", "seq", None), check_vma=False
    )
```
